32 devices in a mesh: groups: 2 (over y), picks: 4 (over z), heads: 4 (over x, core).
Axes of the slice: x: 2, y: 2, z: 4, core: 2. Of those that a mesh axis runs over, the one named last changes fastest.
Arguments:
- coords: float32 [3, 8192], P(None, ('groups', 'picks')), parts along dimension 1, may hold values from -1 to 1
- horizon_ids: int32 [8192], P(('groups', 'picks')), parts along dimension 0, may hold values from 0 to 63
- horizon_levels: float32 [128], P('groups'), parts along dimension 0, may hold values from -2 to 2
- latents: bfloat16 [512, 1024], replicated, may hold values from -960 to 960
- kv_weight: bfloat16 [3072, 2, 1024], P('picks', None, 'heads'), may hold values from -0.109375 to 0.109375
- cross_out: bfloat16 [1024, 1024], P('heads'), may hold values from -0.75 to 0.75
- norm_gains: float32 [2, 1024], replicated, may hold values from 0.1 to 1.9
- self_qkv: bfloat16 [3, 1024, 1024], P(None, None, 'heads'), may hold values from -0.1875 to 0.1875
- self_out: bfloat16 [1024, 1024], P(None, 'heads'), may hold values from -0.1875 to 0.1875
- dec_kv: bfloat16 [2, 1024, 1024], P(None, None, 'heads'), may hold values from -0.1875 to 0.1875
- dec_query: bfloat16 [3072, 1024], P('picks', 'heads'), may hold values from -0.109375 to 0.109375
- readout: float32 [1024], P('heads'), may hold values from -0.1875 to 0.1875
Outputs:
- field: float32 [8192], P(('groups', 'picks')), parts along dimension 0
- latents_out: float32 [1024, 1024], P('groups', 'heads'), parts along dimension 0
- grad_query: float32 [6144, 1024], P(('groups', 'picks'), 'heads'), parts along dimension 0
The draws below stay inside these ranges and needn't reach their ends.
There are 2 independent parts, one for each index of `groups`. The reference program is written for one: setup_inputs(seed, part) draws one part's arguments, and reference() takes and returns one part's arrays. A program takes and returns all parts, laid end to end along the dimension named above; an argument that names none is the same for every part. Nothing has to cross between parts.
All inputs are finite; a program needn't handle non-finite values.
Results may differ from the reference program's by a relative error of at most 0.028.
Values may be sent and summed in bfloat16 or wider, within the bound.
A program may use at most 64 MiB of HBM per device.

```python
import jax
import jax.numpy as jnp
from jax import lax

D = 1024
HEAD = 128
LAT = 512
BANDS = 512
HORIZONS = 64
TOK_DEV = 1024
TOKENS = 4096
ENC = 3072
HEADS = 8


def draw_latents(key, part):
    base = jnp.clip(jax.random.normal(key, (LAT, D), jnp.float32), -6.0, 6.0)
    return base.astype(jnp.bfloat16)


def place_ends(drawn, stream_key, smallest, high):
    shape = drawn.shape
    spot = [jax.random.randint(jax.random.fold_in(stream_key, axis), (), 0, shape[axis]) for axis in range(len(shape))]
    drawn = drawn.at[tuple(spot)].set(smallest)
    longest = shape.index(max(shape))
    spot[longest] = (spot[longest] + 1) % shape[longest]
    return drawn.at[tuple(spot)].set(high)


def levels(own_key, extent, shards, low, top_value):
    def one(dim, parts):
        draws = jax.random.uniform(jax.random.fold_in(jax.random.fold_in(own_key, 6), dim), (parts,), jnp.float32, low / len(shards), top_value / len(shards))
        return jnp.repeat(jnp.exp(draws), extent[dim] // parts).reshape((-1,) + (1,) * (len(extent) - dim - 1))

    factor_of = one(*shards[0])
    for cut in shards[1:]:
        factor_of = factor_of * one(*cut)
    return factor_of


def bell_draw(stream_key, dims, deviation, limit, shards=(), held_as=jnp.bfloat16):
    array = deviation * jax.random.normal(stream_key, dims, jnp.float32)
    if shards:
        array = array * levels(stream_key, dims, shards, -0.22, 0.18)
    return jnp.clip(array, -limit, limit).astype(held_as)


def setup_inputs(seed: int = 0, part: int = 0) -> dict:
    seeds = jax.random.split(jax.random.key(seed), 13)
    own_keys = jax.random.split(jax.random.fold_in(seeds[12], part), 13)
    coords = jnp.clip(jax.random.uniform(own_keys[0], (3, TOKENS), jnp.float32, -1.0, 1.0) * levels(own_keys[0], (3, TOKENS), ((1, 4),), -0.4, 0.0), -1.0, 1.0)
    horizon_ids = place_ends(jax.random.randint(own_keys[1], (TOKENS,), 0, HORIZONS), jax.random.fold_in(own_keys[1], 1), 0, HORIZONS - 1).astype(jnp.int32)
    horizon_levels = jnp.clip(jax.random.uniform(own_keys[2], (HORIZONS,), jnp.float32, -2.0, 2.0), -2.0, 2.0)
    latents = draw_latents(jax.random.fold_in(seeds[12], 71), part)
    kv_weight = bell_draw(seeds[4], (ENC, 2, D), ENC ** -0.5, 0.109375, ((0, 4), (2, 4)))
    cross_out = bell_draw(seeds[5], (D, D), (D // 16) ** -0.5, 0.75, ((0, 4),))
    norm_gains = jnp.clip(1.0 + 0.18 * jax.random.normal(seeds[6], (2, D), jnp.float32), 0.1, 1.9)
    self_qkv = bell_draw(seeds[7], (3, D, D), D ** -0.5, 0.1875, ((2, 4),))
    self_out = bell_draw(seeds[8], (D, D), D ** -0.5, 0.1875, ((1, 4),))
    dec_kv = bell_draw(seeds[9], (2, D, D), D ** -0.5, 0.1875, ((2, 4),))
    dec_query = bell_draw(seeds[10], (ENC, D), ENC ** -0.5, 0.109375, ((0, 4), (1, 4)))
    readout = bell_draw(seeds[11], (D,), D ** -0.5, 0.1875, ((0, 4),), jnp.float32)
    return {"coords": coords, "horizon_ids": horizon_ids, "horizon_levels": horizon_levels, "latents": latents, "kv_weight": kv_weight, "cross_out": cross_out, "norm_gains": norm_gains, "self_qkv": self_qkv, "self_out": self_out, "dec_kv": dec_kv, "dec_query": dec_query, "readout": readout}


PI = 3.141592653589793
EPS = 1e-06

def encode(coords):
    freq = jnp.linspace(1.0, BANDS / 2.0, BANDS).astype(jnp.float32)
    angle = PI * freq[None, :, None] * coords[:, None, :]
    table = jnp.concatenate([jnp.sin(angle), jnp.cos(angle)], axis=0)
    return table.reshape(6 * BANDS, coords.shape[1]).T.astype(jnp.bfloat16)

def rms_norm(state, gain):
    power = lax.optimization_barrier(jnp.mean(state * state, axis=1, keepdims=True))
    return (state * lax.rsqrt(power + EPS) * gain[None, :]).astype(jnp.bfloat16)

def reference(coords, horizon_ids, horizon_levels, latents, kv_weight, cross_out, norm_gains, self_qkv, self_out, dec_kv, dec_query, readout):
    high = lax.Precision.HIGHEST
    scale = HEAD ** (-0.5)
    blocks = TOKENS // TOK_DEV
    enc = encode(coords)
    keys_vals = jnp.dot(enc, kv_weight.reshape(ENC, 2 * D), preferred_element_type=jnp.float32).astype(jnp.bfloat16)
    keys = keys_vals[:, :D].reshape(TOKENS, HEADS, HEAD).transpose(1, 0, 2)
    values = keys_vals[:, D:].reshape(TOKENS, HEADS, HEAD).transpose(1, 0, 2)
    queries = latents.reshape(LAT, HEADS, HEAD).transpose(1, 0, 2)

    def cross_head(items):
        query_h, key_h, value_h = items
        scores = jnp.dot(query_h, key_h.T, preferred_element_type=jnp.float32) * scale
        scores = scores.reshape(LAT, blocks, TOK_DEV)
        top = lax.optimization_barrier(jnp.max(scores, axis=2))
        expo = jnp.exp(scores - top[:, :, None])
        total = lax.optimization_barrier(jnp.sum(expo, axis=2))
        rounded = lax.optimization_barrier(expo.astype(jnp.bfloat16)).astype(jnp.float32)
        part = jnp.einsum('lbt,btc->lbc', rounded, value_h.reshape(blocks, TOK_DEV, HEAD).astype(jnp.float32), precision=high)
        best = lax.optimization_barrier(jnp.max(top, axis=1, keepdims=True))
        factor = jnp.exp(top - best)
        numer = lax.optimization_barrier(jnp.sum(part * factor[:, :, None], axis=1))
        return numer / lax.optimization_barrier(jnp.sum(total * factor, axis=1))[:, None]
    attended = lax.map(cross_head, (queries, keys, values))
    attended = attended.transpose(1, 0, 2).reshape(LAT, D).astype(jnp.bfloat16)
    state = latents.astype(jnp.float32) + jnp.dot(attended, cross_out, preferred_element_type=jnp.float32)
    normed = rms_norm(state, norm_gains[0])
    qkv = jnp.einsum('ld,kde->kle', normed.astype(jnp.float32), self_qkv.astype(jnp.float32), precision=high).astype(jnp.bfloat16)
    sq = qkv[0].reshape(LAT, HEADS, HEAD).astype(jnp.float32)
    sk = qkv[1].reshape(LAT, HEADS, HEAD).astype(jnp.float32)
    sv = qkv[2].reshape(LAT, HEADS, HEAD).astype(jnp.float32)
    scores = jnp.einsum('lhc,mhc->hlm', sq, sk, precision=high) * scale
    expo = jnp.exp(scores)
    probs = (expo / lax.optimization_barrier(jnp.sum(expo, axis=2, keepdims=True))).astype(jnp.bfloat16)
    head_out = jnp.einsum('hlm,mhc->lhc', probs.astype(jnp.float32), sv, precision=high).astype(jnp.bfloat16).reshape(LAT, D)
    latents_out = state + jnp.dot(head_out, self_out, preferred_element_type=jnp.float32)
    normed2 = rms_norm(latents_out, norm_gains[1])
    dec = jnp.einsum('ld,kde->kle', normed2.astype(jnp.float32), dec_kv.astype(jnp.float32), precision=high).astype(jnp.bfloat16)
    dec_keys = dec[0].reshape(LAT, HEADS, HEAD).astype(jnp.float32)
    dec_vals = dec[1].reshape(LAT, HEADS, HEAD).astype(jnp.float32)
    query = jnp.dot(enc, dec_query, preferred_element_type=jnp.float32).astype(jnp.bfloat16)
    onehot = (horizon_ids[:, None] == jnp.arange(HORIZONS, dtype=jnp.int32)[None, :]).astype(jnp.float32)
    target = lax.optimization_barrier(jnp.sum(onehot * horizon_levels[None, :], axis=1))
    read = readout.reshape(HEADS, HEAD)
    value_read = jnp.einsum('lhc,hc->hl', dec_vals, read, precision=high)

    def decode(items):
        query_b, target_b = items
        dq = query_b.reshape(TOK_DEV, HEADS, HEAD).astype(jnp.float32)
        sc = jnp.einsum('thc,lhc->htl', dq, dec_keys, precision=high) * scale
        ex = jnp.exp(sc)
        weights = ex / lax.optimization_barrier(jnp.sum(ex, axis=2, keepdims=True))
        rounded = lax.optimization_barrier(weights.astype(jnp.bfloat16)).astype(jnp.float32)
        out = jnp.einsum('htl,lhc->thc', rounded, dec_vals, precision=high)
        field_b = lax.optimization_barrier(jnp.sum(out * read[None, :, :], axis=(1, 2)))
        miss = field_b - target_b
        dprob = miss[None, :, None] * value_read[:, None, :]
        dscore = weights * (dprob - lax.optimization_barrier(jnp.sum(dprob * weights, axis=2, keepdims=True)))
        dscore = lax.optimization_barrier(dscore.astype(jnp.bfloat16)).astype(jnp.float32)
        dquery = jnp.einsum('htl,lhc->thc', dscore, dec_keys, precision=high) * scale
        return (field_b, dquery.reshape(TOK_DEV, D).astype(jnp.bfloat16))
    field, dquery = lax.map(decode, (query.reshape(blocks, TOK_DEV, D), target.reshape(blocks, TOK_DEV)))
    grad_query = jnp.dot(enc.T, dquery.reshape(TOKENS, D), preferred_element_type=jnp.float32)
    return (field.reshape(TOKENS), latents_out, grad_query)
```

```python
import functools

import jax
import jax.numpy as jnp
from jax import lax
from jax.experimental import pallas as pl
from jax.experimental.pallas import tpu as pltpu
from jax.sharding import PartitionSpec as P

HEAD = 128
BANDS = 512
HORIZONS = 64
PI = 3.141592653589793
EPS = 1e-06
F32 = jnp.float32
BF16 = jnp.bfloat16
LAST = (((1,), (1,)), ((), ()))


def sin_half(r):
    u = r * r
    p = 0.07765766 * u - 0.5982913
    p = p * u + 2.55007753
    p = p * u - 5.16771008
    p = p * u + PI
    return p * r


def cos_half(r):
    u = r * r
    p = -0.02439632 * u + 0.23493732
    p = p * u - 1.335212
    p = p * u + 4.05870916
    p = p * u - 4.93480214
    return p * u + 1.0


def kernel(
    npick, nhead,
    coords_ref, ids_ref, levels_ref, freq_ref, latents_ref, kv_in, cross_in, gains_ref,
    qkvw_ref, sout_in, deckv_ref, dq_in, readout_ref,
    field_ref, latout_ref, grad_ref,
    enc, kvw, dqw, cross, sout, kvs, numer, stats, stin, parts, coef, coeft, att, state,
    qkv, heads_all, dkeys, dkeyst, vread, query, dqt, dqb, fpart, fin, gbuf, gin,
    kv_s, kv_r, kvy_s, kvy_r, dq_s, dq_r, dqy_s, dqy_r, cr_s, cr_r, so_s, so_r,
    nu_s, nu_r, st_s, st_r, az_s, az_r, ah_s, ah_r, ho_s, ho_r, fd_s, fd_r, gr_s, gr_r, loc,
):
    g = lax.axis_index("groups")
    p = lax.axis_index("picks")
    hd = lax.axis_index("heads")
    mate = {"groups": 1 - g}
    scale = HEAD ** (-0.5)
    count, features = enc.shape
    lat_rows, width = latents_ref.shape
    rows = dq_in.shape[0]
    half = rows // 2
    local = dq_in.shape[1]
    nh = local // HEAD
    share = lat_rows // npick
    col = pl.multiple_of(hd * local, HEAD)
    sends = []

    def put(src, dst, ssem, rsem, to):
        return pltpu.make_async_remote_copy(
            src_ref=src, dst_ref=dst, send_sem=ssem, recv_sem=rsem, device_id=to,
            device_id_type=pl.DeviceIdType.MESH,
        )

    def go(copy):
        copy.start()
        sends.append(copy)
        return copy

    zto = [None] + [{"picks": lax.rem(p + d, npick)} for d in range(1, npick)]
    zfrom = [p] + [lax.rem(p + npick - d, npick) for d in range(1, npick)]
    hto = [None] + [{"heads": lax.rem(hd + e, nhead)} for e in range(1, nhead)]

    own = []
    mine = pl.multiple_of(p * rows, 16)
    own.append(pltpu.make_async_copy(kv_in, kvw.at[pl.ds(mine, rows)], loc.at[0]))
    own.append(pltpu.make_async_copy(dq_in, dqw.at[pl.ds(mine, rows)], loc.at[1]))
    own.append(pltpu.make_async_copy(cross_in, cross.at[pl.ds(col, local)], loc.at[2]))
    own.append(pltpu.make_async_copy(sout_in, sout.at[:, pl.ds(col, local)], loc.at[3]))
    for c in own:
        c.start()

    barrier = pltpu.get_barrier_semaphore()
    for to in zto[1:] + hto[1:] + [mate]:
        pl.semaphore_signal(barrier, inc=1, device_id=to, device_id_type=pl.DeviceIdType.MESH)
    pl.semaphore_wait(barrier, npick + nhead - 1)

    myhalf = pl.multiple_of(g * half, 16)
    dst_half = pl.ds(pl.multiple_of(p * rows + g * half, 16), half)
    kvz = [None] + [
        go(put(kv_in.at[pl.ds(myhalf, half)], kvw.at[dst_half], kv_s.at[d], kv_r.at[d], zto[d]))
        for d in range(1, npick)
    ]
    crh = [
        go(put(cross_in, cross.at[pl.ds(col, local)], cr_s.at[e], cr_r.at[e], hto[e]))
        for e in range(1, nhead)
    ]
    soh = [
        go(put(sout_in, sout.at[:, pl.ds(col, local)], so_s.at[e], so_r.at[e], hto[e]))
        for e in range(1, nhead)
    ]
    dqz = [None] + [
        go(put(dq_in.at[pl.ds(myhalf, half)], dqw.at[dst_half], dq_s.at[d], dq_r.at[d], zto[d]))
        for d in range(1, npick)
    ]

    tile = 32
    freq = freq_ref[...]

    def encode(i, _):
        at = pl.ds(pl.multiple_of(i * tile, tile), tile)
        for c in range(3):
            turn = coords_ref[at, c : c + 1] * freq
            r = turn - jnp.floor(turn + 0.5)
            s = sin_half(r)
            k = cos_half(r)
            enc[at, c * BANDS : (c + 1) * BANDS] = (2.0 * s * k).astype(BF16)
            enc[at, (3 + c) * BANDS : (4 + c) * BANDS] = (1.0 - 2.0 * s * s).astype(BF16)
        return 0

    lax.fori_loop(0, count // tile, encode, 0)

    kvy = []
    for d in range(1, npick):
        kvz[d].wait_recv()
        at = pl.ds(pl.multiple_of(zfrom[d] * rows + g * half, 16), half)
        kvy.append(go(put(kvw.at[at], kvw.at[at], kvy_s.at[d], kvy_r.at[d], mate)))
    own[0].wait()
    for c in kvy:
        c.wait_recv()

    def keys_values(i, _):
        at = pl.ds(pl.multiple_of(i * 256, 256), 256)
        kvs[at, :] = jnp.dot(enc[at, :], kvw[...], preferred_element_type=F32).astype(BF16)
        return 0

    lax.fori_loop(0, count // 256, keys_values, 0)

    lane = lax.broadcasted_iota(jnp.int32, (128, 128), 1)

    def cross_attention(i, _):
        at = pl.ds(pl.multiple_of(i * 128, 128), 128)
        mark = jnp.zeros((128, 128), F32)
        for h in range(nh):
            q = latents_ref[at, pl.ds(pl.multiple_of(col + h * HEAD, HEAD), HEAD)]
            s = lax.dot_general(q, kvs[:, h * HEAD : (h + 1) * HEAD], LAST, preferred_element_type=F32) * scale
            top = jnp.max(s, axis=1, keepdims=True)
            e = jnp.exp(s - top)
            total = jnp.sum(e, axis=1, keepdims=True)
            numer[at, h * HEAD : (h + 1) * HEAD] = jnp.dot(
                e.astype(BF16), kvs[:, local + h * HEAD : local + (h + 1) * HEAD], preferred_element_type=F32
            ).astype(BF16)
            mark = jnp.where(lane == 2 * h, top, jnp.where(lane == 2 * h + 1, total, mark))
        stats[at, :] = mark
        return 0

    lax.fori_loop(0, lat_rows // 128, cross_attention, 0)
    stin[0] = stats[...].T[:8]
    stz, nuz = [None], [None]
    for d in range(1, npick):
        dst = lax.rem(p + d, npick)
        stz.append(go(put(stin.at[0], stin.at[d], st_s.at[d], st_r.at[d], zto[d])))
        nuz.append(go(put(
            numer.at[pl.ds(pl.multiple_of(dst * share, 16), share)], parts.at[d],
            nu_s.at[d], nu_r.at[d], zto[d],
        )))
    dqy = []
    for d in range(1, npick):
        dqz[d].wait_recv()
        at = pl.ds(pl.multiple_of(zfrom[d] * rows + g * half, 16), half)
        dqy.append(go(put(dqw.at[at], dqw.at[at], dqy_s.at[d], dqy_r.at[d], mate)))
    for d in range(1, npick):
        stz[d].wait_recv()
    coef[...] = jnp.zeros(coef.shape, F32)
    for h in range(nh):
        best = stin[0, 2 * h : 2 * h + 1, :]
        for d in range(1, npick):
            best = jnp.maximum(best, stin[d, 2 * h : 2 * h + 1, :])
        factors = [jnp.exp(stin[d, 2 * h : 2 * h + 1, :] - best) for d in range(npick)]
        total = sum(factors[d] * stin[d, 2 * h + 1 : 2 * h + 2, :] for d in range(npick))
        for d in range(npick):
            coef[2 * d + h : 2 * d + h + 1, :] = factors[d] / total
    coeft[...] = coef[...].T
    myrows = pl.ds(pl.multiple_of(p * share, 16), share)
    factor = coeft[myrows, :]
    for d in range(1, npick):
        nuz[d].wait_recv()
    for h in range(nh):
        cols = slice(h * HEAD, (h + 1) * HEAD)
        acc = numer[myrows, cols].astype(F32) * factor[:, h : h + 1]
        for d in range(1, npick):
            acc += parts[d, :, cols].astype(F32) * factor[:, 2 * d + h : 2 * d + h + 1]
        att[myrows, pl.ds(pl.multiple_of(col + h * HEAD, HEAD), HEAD)] = acc.astype(BF16)
    mycols = pl.ds(col, local)
    azz = [None] + [
        go(put(att.at[myrows, mycols], att.at[myrows, mycols], az_s.at[d], az_r.at[d], zto[d]))
        for d in range(1, npick)
    ]
    ahh = []
    for d in range(npick):
        if d:
            azz[d].wait_recv()
        at = pl.ds(pl.multiple_of(zfrom[d] * share, 16), share)
        for e in range(1, nhead):
            k = d * nhead + e
            ahh.append(go(put(att.at[at, mycols], att.at[at, mycols], ah_s.at[k], ah_r.at[k], hto[e])))
    own[1].wait()
    for c in dqy:
        c.wait_recv()

    def queries(i, _):
        at = pl.ds(pl.multiple_of(i * 256, 256), 256)
        query[at, :] = jnp.dot(enc[at, :], dqw[...], preferred_element_type=F32).astype(BF16)
        return 0

    lax.fori_loop(0, count // 256, queries, 0)
    own[2].wait()
    for c in crh + ahh:
        c.wait_recv()

    def layer_in(i, _):
        at = pl.ds(pl.multiple_of(i * 128, 128), 128)
        x = latents_ref[at, :].astype(F32) + jnp.dot(att[at, :], cross[...], preferred_element_type=F32)
        state[at, :] = x
        power = jnp.mean(x * x, axis=1, keepdims=True)
        normed = (x * lax.rsqrt(power + EPS) * gains_ref[0:1, :]).astype(BF16)
        for j in range(3):
            qkv[j, at, :] = jnp.dot(normed, qkvw_ref[j], preferred_element_type=F32).astype(BF16)
        return 0

    lax.fori_loop(0, lat_rows // 128, layer_in, 0)

    def self_attention(i, _):
        at = pl.ds(pl.multiple_of(i * 128, 128), 128)
        for h in range(nh):
            cols = slice(h * HEAD, (h + 1) * HEAD)
            s = lax.dot_general(qkv[0, at, cols], qkv[1, :, cols], LAST, preferred_element_type=F32) * scale
            e = jnp.exp(s)
            probs = (e * (1.0 / jnp.sum(e, axis=1, keepdims=True))).astype(BF16)
            heads_all[at, pl.ds(pl.multiple_of(col + h * HEAD, HEAD), HEAD)] = jnp.dot(
                probs, qkv[2, :, cols], preferred_element_type=F32
            ).astype(BF16)
        return 0

    lax.fori_loop(0, lat_rows // 128, self_attention, 0)
    hoh = [
        go(put(heads_all.at[:, mycols], heads_all.at[:, mycols], ho_s.at[e], ho_r.at[e], hto[e]))
        for e in range(1, nhead)
    ]
    horizon = lax.broadcasted_iota(jnp.int32, (HORIZONS, count), 0)
    target = jnp.sum(jnp.where(horizon == ids_ref[...], levels_ref[...], 0.0), axis=0, keepdims=True)
    own[3].wait()
    for c in soh + hoh:
        c.wait_recv()

    def layer_out(i, _):
        at = pl.ds(pl.multiple_of(i * 128, 128), 128)
        x = state[at, :] + jnp.dot(heads_all[at, :], sout[...], preferred_element_type=F32)
        state[at, :] = x
        power = jnp.mean(x * x, axis=1, keepdims=True)
        normed = (x * lax.rsqrt(power + EPS) * gains_ref[1:2, :]).astype(BF16)
        dkeys[at, :] = jnp.dot(normed, deckv_ref[0], preferred_element_type=F32).astype(BF16)
        vals = jnp.dot(normed, deckv_ref[1], preferred_element_type=F32).astype(BF16).astype(F32)
        vals = vals * readout_ref[...]
        mark = jnp.zeros((128, 128), F32)
        for h in range(nh):
            mark = jnp.where(
                lane == h, jnp.sum(vals[:, h * HEAD : (h + 1) * HEAD], axis=1, keepdims=True), mark
            )
        vread[at, :] = mark
        return 0

    lax.fori_loop(0, lat_rows // 128, layer_out, 0)
    latout_ref[...] = state[:, mycols]
    dkeyst[...] = dkeys[...].astype(F32).T.astype(BF16)

    def decode(i, _):
        at = pl.ds(pl.multiple_of(i * 256, 256), 256)
        mine = jnp.zeros((1, 256), F32)
        for h in range(nh):
            cols = slice(h * HEAD, (h + 1) * HEAD)
            s = lax.dot_general(dkeys[:, cols], query[at, cols], LAST, preferred_element_type=F32) * scale
            e = jnp.exp(s)
            w = e * (1.0 / jnp.sum(e, axis=0, keepdims=True))
            v = vread[:, h : h + 1]
            f = jnp.sum(w * v, axis=0, keepdims=True)
            mine += f
            dqt[cols, at] = jnp.dot(
                dkeyst[cols, :], (w * (v - f)).astype(BF16), preferred_element_type=F32
            )
        fpart[:, at] = jnp.broadcast_to(mine, (8, 256))
        return 0

    lax.fori_loop(0, count // 256, decode, 0)
    fdh = [
        go(put(fpart, fin.at[e], fd_s.at[e], fd_r.at[e], hto[e])) for e in range(1, nhead)
    ]
    for c in fdh:
        c.wait_recv()
    field = fpart[0:1, :]
    for e in range(1, nhead):
        field = field + fin[e, 0:1, :]
    field_ref[...] = field
    dqb[...] = (dqt[...] * ((field - target) * scale)).astype(BF16)

    def gradient(i, _):
        at = pl.ds(pl.multiple_of(i * 512, 512), 512)
        out = jnp.dot(dqb[...], enc[:, at], preferred_element_type=F32)
        gbuf[at, :] = out.T.astype(BF16)
        return 0

    lax.fori_loop(0, features // 512, gradient, 0)
    grz = [
        go(put(
            gbuf.at[pl.ds(pl.multiple_of(lax.rem(p + d, npick) * rows, 16), rows)], gin.at[d],
            gr_s.at[d], gr_r.at[d], zto[d],
        ))
        for d in range(1, npick)
    ]
    for c in grz:
        c.wait_recv()
    total = gbuf[pl.ds(mine, rows), :].astype(F32)
    for d in range(1, npick):
        total += gin[d].astype(F32)
    grad_ref[...] = total
    for c in sends:
        c.wait_send()


def on_device(
    npick, nhead, coords, horizon_ids, horizon_levels, latents, kv_weight, cross_out, norm_gains,
    self_qkv, self_out, dec_kv, dec_query, readout,
):
    count = coords.shape[1]
    rows, local = dec_query.shape
    lat_rows, width = latents.shape
    features = rows * npick
    share = lat_rows // npick
    wide = -(-2 * npick // 128) * 128
    freq = (0.5 * jnp.linspace(1.0, BANDS / 2.0, BANDS).astype(F32)).reshape(1, BANDS)
    vmem = pl.BlockSpec(memory_space=pltpu.VMEM)
    hbm = pl.BlockSpec(memory_space=pl.ANY)
    dma = lambda n: pltpu.SemaphoreType.DMA((n,))
    scratch = [
        pltpu.VMEM((count, features), BF16),
        pltpu.VMEM((features, 2 * local), BF16),
        pltpu.VMEM((features, local), BF16),
        pltpu.VMEM((width, width), BF16),
        pltpu.VMEM((width, width), BF16),
        pltpu.VMEM((count, 2 * local), BF16),
        pltpu.VMEM((lat_rows, local), BF16),
        pltpu.VMEM((lat_rows, 128), F32),
        pltpu.VMEM((npick, 8, lat_rows), F32),
        pltpu.VMEM((npick, share, local), BF16),
        pltpu.VMEM((wide, lat_rows), F32),
        pltpu.VMEM((lat_rows, wide), F32),
        pltpu.VMEM((lat_rows, width), BF16),
        pltpu.VMEM((lat_rows, width), F32),
        pltpu.VMEM((3, lat_rows, local), BF16),
        pltpu.VMEM((lat_rows, width), BF16),
        pltpu.VMEM((lat_rows, local), BF16),
        pltpu.VMEM((local, lat_rows), BF16),
        pltpu.VMEM((lat_rows, 128), F32),
        pltpu.VMEM((count, local), BF16),
        pltpu.VMEM((local, count), F32),
        pltpu.VMEM((local, count), BF16),
        pltpu.VMEM((8, count), F32),
        pltpu.VMEM((nhead, 8, count), F32),
        pltpu.VMEM((features, local), BF16),
        pltpu.VMEM((npick, rows, local), BF16),
    ]
    z, h = npick, nhead
    for n in (z, z, z, z, h, h, z, z, z, z * h, h, h, z):
        scratch += [dma(n), dma(n)]
    scratch.append(dma(4))
    field, latents_out, grad = pl.pallas_call(
        functools.partial(kernel, npick, nhead),
        out_shape=(
            jax.ShapeDtypeStruct((1, count), F32),
            jax.ShapeDtypeStruct((lat_rows, local), F32),
            jax.ShapeDtypeStruct((rows, local), F32),
        ),
        in_specs=[vmem] * 5 + [hbm, hbm, vmem, vmem, hbm, vmem, hbm, vmem],
        out_specs=(vmem, vmem, vmem),
        scratch_shapes=scratch,
        compiler_params=pltpu.CompilerParams(
            collective_id=0, has_side_effects=True, vmem_limit_bytes=56 * 2**20
        ),
    )(
        coords.T,
        horizon_ids.reshape(1, count),
        horizon_levels.reshape(-1, 1),
        freq,
        latents,
        kv_weight.reshape(rows, 2 * local),
        cross_out,
        norm_gains,
        self_qkv,
        self_out,
        dec_kv,
        dec_query,
        readout.reshape(1, local),
    )
    return field.reshape(count), latents_out, grad


def solution(mesh):
    in_specs = (
        P(None, ("groups", "picks")),
        P(("groups", "picks")),
        P("groups"),
        P(),
        P("picks", None, "heads"),
        P("heads", None),
        P(),
        P(None, None, "heads"),
        P(None, "heads"),
        P(None, None, "heads"),
        P("picks", "heads"),
        P("heads"),
    )
    out_specs = (P(("groups", "picks")), P("groups", "heads"), P(("groups", "picks"), "heads"))
    return jax.shard_map(
        functools.partial(on_device, mesh.shape["picks"], mesh.shape["heads"]),
        mesh=mesh, in_specs=in_specs, out_specs=out_specs, check_vma=False,
    )
```

```python
import functools

import jax
import jax.numpy as jnp
from jax import lax
from jax.experimental import pallas as pl
from jax.experimental.pallas import tpu as pltpu
from jax.sharding import PartitionSpec as P

HEAD = 128
BANDS = 512
HORIZONS = 64
PI = 3.141592653589793
EPS = 1e-06
F32 = jnp.float32
BF16 = jnp.bfloat16
LAST = (((1,), (1,)), ((), ()))


def sin_half(r):
    u = r * r
    p = 0.07765766 * u - 0.5982913
    p = p * u + 2.55007753
    p = p * u - 5.16771008
    p = p * u + PI
    return p * r


def cos_half(r):
    u = r * r
    p = -0.02439632 * u + 0.23493732
    p = p * u - 1.335212
    p = p * u + 4.05870916
    p = p * u - 4.93480214
    return p * u + 1.0


def kernel(
    npick, nhead,
    coords_ref, ids_ref, levels_ref, freq_ref, latents_ref, kv_in, cross_in, gains_ref,
    qkvw_ref, sout_in, deckv_ref, dq_in, readout_ref,
    field_ref, latout_ref, grad_ref,
    enc, kvw, dqw, cross, sout, kvs, numer, stats, stin, parts, coef, coeft, att, state,
    qkv, heads_all, dkeys, dkeyst, vread, query, dqt, dqb, fpart, fin, gbuf, gin, gin_left, expo,
    wz_s, wz_r, wy_s, wy_r, cr_s, cr_r, so_s, so_r,
    nu_s, nu_r, st_s, st_r, az_s, az_r, ah_s, ah_r, ho_s, ho_r, fd_s, fd_r, gr_s, gr_r, gl_r, loc,
):
    g = lax.axis_index("groups")
    p = lax.axis_index("picks")
    hd = lax.axis_index("heads")
    mate = {"groups": 1 - g}
    scale = HEAD ** (-0.5)
    count, features = enc.shape
    lat_rows, width = latents_ref.shape
    rows = dq_in.shape[0]
    half = rows // 2
    local = dq_in.shape[1]
    nh = local // HEAD
    share = lat_rows // npick
    col = pl.multiple_of(hd * local, HEAD)
    sends = []

    def put(src, dst, ssem, rsem, to):
        return pltpu.make_async_remote_copy(
            src_ref=src, dst_ref=dst, send_sem=ssem, recv_sem=rsem, device_id=to,
            device_id_type=pl.DeviceIdType.MESH,
        )

    def go(copy):
        copy.start()
        sends.append(copy)
        return copy

    zto = [None] + [{"picks": lax.rem(p + d, npick)} for d in range(1, npick)]
    zfrom = [p] + [lax.rem(p + npick - d, npick) for d in range(1, npick)]
    hto = [None] + [{"heads": lax.rem(hd + e, nhead)} for e in range(1, nhead)]

    own = []
    mine = pl.multiple_of(p * rows, 16)
    own.append(pltpu.make_async_copy(kv_in, kvw.at[pl.ds(mine, rows)], loc.at[0]))
    own.append(pltpu.make_async_copy(dq_in, dqw.at[pl.ds(mine, rows)], loc.at[1]))
    own.append(pltpu.make_async_copy(cross_in, cross.at[pl.ds(col, local)], loc.at[2]))
    own.append(pltpu.make_async_copy(sout_in, sout.at[:, pl.ds(col, local)], loc.at[3]))
    for c in own:
        c.start()

    barrier = pltpu.get_barrier_semaphore()
    for to in zto[1:] + hto[1:] + [mate]:
        pl.semaphore_signal(barrier, inc=1, device_id=to, device_id_type=pl.DeviceIdType.MESH)
    pl.semaphore_wait(barrier, npick + nhead - 1)

    spots = [(kv_in, kvw, 0), (kv_in, kvw, local), (dq_in, dqw, 0)]
    ahead = [{"picks": jnp.minimum(p + 1, npick - 1)}, {"picks": jnp.maximum(p - 1, 0)}]
    may = [p + 1 < npick, p > 0]

    def span(owner, part):
        return pl.ds(pl.multiple_of(owner * rows + part * half, 16), half)

    def along(c, way, s):
        _, whole, first = spots[c]
        owner = p - s if way == 0 else p + s
        ref = whole.at[span(owner, g), pl.ds(first, local)]
        k = (c * 2 + way) * npick + s
        return put(ref, ref, wz_s.at[k], wz_r.at[k + 1], ahead[way])

    def start_own(c):
        source, whole, first = spots[c]
        for way in range(2):
            k = (c * 2 + way) * npick

            @pl.when(may[way])
            def _():
                put(
                    source.at[pl.ds(pl.multiple_of(g * half, 16), half), pl.ds(first, local)],
                    whole.at[span(p, g), pl.ds(first, local)],
                    wz_s.at[k], wz_r.at[k + 1], ahead[way],
                ).start()

    def across(c, way, s):
        _, whole, first = spots[c]
        owner = p - s if way == 0 else p + s
        ref = whole.at[span(owner, g), pl.ds(first, local)]
        k = (c * 2 + way) * npick + s
        return put(ref, ref, wy_s.at[k], wy_r.at[k], mate)

    def has(way, s):
        return p - s >= 0 if way == 0 else p + s < npick

    def pass_on(c, s):
        _, whole, first = spots[c]
        for way in range(2):

            @pl.when(has(way, s))
            def _():
                owner = p - s if way == 0 else p + s
                ref = whole.at[span(owner, g), pl.ds(first, local)]
                k = (c * 2 + way) * npick + s
                put(ref, ref, wz_s.at[k], wz_r.at[k], mate).wait_recv()
                across(c, way, s).start()

                if s < npick - 1:

                    @pl.when(may[way])
                    def _():
                        along(c, way, s).start()

    def pass_on_rest(c):
        for s in range(3, npick):
            pass_on(c, s)

    def arrive(c):
        for s in range(1, npick):
            for way in range(2):

                @pl.when(has(way, s))
                def _():
                    across(c, way, s).wait_recv()

    def finish(c):
        for s in range(npick):
            for way in range(2):
                if s < npick - 1:

                    @pl.when(has(way, s) & may[way])
                    def _():
                        along(c, way, s).wait_send()

                if s:

                    @pl.when(has(way, s))
                    def _():
                        across(c, way, s).wait_send()

    start_own(0)
    crh = [
        go(put(cross_in, cross.at[pl.ds(col, local)], cr_s.at[e], cr_r.at[e], hto[e]))
        for e in range(1, nhead)
    ]
    soh = [
        go(put(sout_in, sout.at[:, pl.ds(col, local)], so_s.at[e], so_r.at[e], hto[e]))
        for e in range(1, nhead)
    ]

    tile = 32
    freq = freq_ref[...]

    def encode(i, _):
        at = pl.ds(pl.multiple_of(i * tile, tile), tile)
        for c in range(3):
            turn = coords_ref[at, c : c + 1] * freq
            r = turn - jnp.floor(turn + 0.5)
            s = sin_half(r)
            k = cos_half(r)
            enc[at, c * BANDS : (c + 1) * BANDS] = (2.0 * s * k).astype(BF16)
            enc[at, (3 + c) * BANDS : (4 + c) * BANDS] = (1.0 - 2.0 * s * s).astype(BF16)
        return 0

    steps = count // tile
    lax.fori_loop(0, steps // 3, encode, 0)
    pass_on(0, 1)
    start_own(1)
    lax.fori_loop(steps // 3, 2 * steps // 3, encode, 0)
    if npick > 2:
        pass_on(0, 2)
    lax.fori_loop(2 * steps // 3, steps, encode, 0)
    pass_on_rest(0)
    pass_on(1, 1)
    start_own(2)
    own[0].wait()
    arrive(0)

    def project(first):
        def body(i, _):
            at = pl.ds(pl.multiple_of(i * 256, 256), 256)
            kvs[at, first : first + local] = jnp.dot(
                enc[at, :], kvw[:, first : first + local], preferred_element_type=F32
            ).astype(BF16)
            return 0

        lax.fori_loop(0, count // 256, body, 0)

    project(0)
    if npick > 2:
        pass_on(1, 2)

    lane = lax.broadcasted_iota(jnp.int32, (128, 128), 1)

    def cross_scores(i, _):
        at = pl.ds(pl.multiple_of(i * 128, 128), 128)
        mark = jnp.zeros((128, 128), F32)
        for h in range(nh):
            q = latents_ref[at, pl.ds(pl.multiple_of(col + h * HEAD, HEAD), HEAD)]
            s = lax.dot_general(q, kvs[:, h * HEAD : (h + 1) * HEAD], LAST, preferred_element_type=F32) * scale
            top = jnp.max(s, axis=1, keepdims=True)
            e = jnp.exp(s - top)
            total = jnp.sum(e, axis=1, keepdims=True)
            expo[h, at, :] = e.astype(BF16)
            mark = jnp.where(lane == 2 * h, top, jnp.where(lane == 2 * h + 1, total, mark))
        stats[at, :] = mark
        return 0

    lax.fori_loop(0, lat_rows // 128, cross_scores, 0)
    pass_on_rest(1)
    stin[0] = stats[...].T[:8]
    stz, nuz = [None], [None]
    for d in range(1, npick):
        stz.append(go(put(stin.at[0], stin.at[d], st_s.at[d], st_r.at[d], zto[d])))
    pass_on(2, 1)
    arrive(1)
    project(local)
    if npick > 2:
        pass_on(2, 2)

    def cross_values(i, _):
        at = pl.ds(pl.multiple_of(i * 128, 128), 128)
        for h in range(nh):
            numer[at, h * HEAD : (h + 1) * HEAD] = jnp.dot(
                expo[h, at, :], kvs[:, local + h * HEAD : local + (h + 1) * HEAD], preferred_element_type=F32
            ).astype(BF16)
        return 0

    lax.fori_loop(0, lat_rows // 128, cross_values, 0)
    for d in range(1, npick):
        dst = lax.rem(p + d, npick)
        nuz.append(go(put(
            numer.at[pl.ds(pl.multiple_of(dst * share, 16), share)], parts.at[d],
            nu_s.at[d], nu_r.at[d], zto[d],
        )))
    pass_on_rest(2)
    for d in range(1, npick):
        stz[d].wait_recv()
    coef[...] = jnp.zeros(coef.shape, F32)
    for h in range(nh):
        best = stin[0, 2 * h : 2 * h + 1, :]
        for d in range(1, npick):
            best = jnp.maximum(best, stin[d, 2 * h : 2 * h + 1, :])
        factors = [jnp.exp(stin[d, 2 * h : 2 * h + 1, :] - best) for d in range(npick)]
        total = sum(factors[d] * stin[d, 2 * h + 1 : 2 * h + 2, :] for d in range(npick))
        for d in range(npick):
            coef[2 * d + h : 2 * d + h + 1, :] = factors[d] / total
    coeft[...] = coef[...].T
    myrows = pl.ds(pl.multiple_of(p * share, 16), share)
    factor = coeft[myrows, :]
    for d in range(1, npick):
        nuz[d].wait_recv()
    for h in range(nh):
        cols = slice(h * HEAD, (h + 1) * HEAD)
        acc = numer[myrows, cols].astype(F32) * factor[:, h : h + 1]
        for d in range(1, npick):
            acc += parts[d, :, cols].astype(F32) * factor[:, 2 * d + h : 2 * d + h + 1]
        att[myrows, pl.ds(pl.multiple_of(col + h * HEAD, HEAD), HEAD)] = acc.astype(BF16)
    mycols = pl.ds(col, local)
    azz = [None] + [
        go(put(att.at[myrows, mycols], att.at[myrows, mycols], az_s.at[d], az_r.at[d], zto[d]))
        for d in range(1, npick)
    ]
    ahh = []
    for d in range(npick):
        if d:
            azz[d].wait_recv()
        at = pl.ds(pl.multiple_of(zfrom[d] * share, 16), share)
        for e in range(1, nhead):
            k = d * nhead + e
            ahh.append(go(put(att.at[at, mycols], att.at[at, mycols], ah_s.at[k], ah_r.at[k], hto[e])))
    own[1].wait()
    arrive(2)

    def queries(i, _):
        at = pl.ds(pl.multiple_of(i * 256, 256), 256)
        query[at, :] = jnp.dot(enc[at, :], dqw[...], preferred_element_type=F32).astype(BF16)
        return 0

    lax.fori_loop(0, count // 256, queries, 0)
    own[2].wait()
    for c in crh + ahh:
        c.wait_recv()

    def layer_in(i, _):
        at = pl.ds(pl.multiple_of(i * 128, 128), 128)
        x = latents_ref[at, :].astype(F32) + jnp.dot(att[at, :], cross[...], preferred_element_type=F32)
        state[at, :] = x
        power = jnp.mean(x * x, axis=1, keepdims=True)
        normed = (x * lax.rsqrt(power + EPS) * gains_ref[0:1, :]).astype(BF16)
        for j in range(3):
            qkv[j, at, :] = jnp.dot(normed, qkvw_ref[j], preferred_element_type=F32).astype(BF16)
        return 0

    lax.fori_loop(0, lat_rows // 128, layer_in, 0)

    def self_attention(i, _):
        at = pl.ds(pl.multiple_of(i * 128, 128), 128)
        for h in range(nh):
            cols = slice(h * HEAD, (h + 1) * HEAD)
            s = lax.dot_general(qkv[0, at, cols], qkv[1, :, cols], LAST, preferred_element_type=F32) * scale
            e = jnp.exp(s)
            probs = (e * (1.0 / jnp.sum(e, axis=1, keepdims=True))).astype(BF16)
            heads_all[at, pl.ds(pl.multiple_of(col + h * HEAD, HEAD), HEAD)] = jnp.dot(
                probs, qkv[2, :, cols], preferred_element_type=F32
            ).astype(BF16)
        return 0

    lax.fori_loop(0, lat_rows // 128, self_attention, 0)
    hoh = [
        go(put(heads_all.at[:, mycols], heads_all.at[:, mycols], ho_s.at[e], ho_r.at[e], hto[e]))
        for e in range(1, nhead)
    ]
    horizon = lax.broadcasted_iota(jnp.int32, (HORIZONS, count), 0)
    target = jnp.sum(jnp.where(horizon == ids_ref[...], levels_ref[...], 0.0), axis=0, keepdims=True)
    own[3].wait()
    for c in soh + hoh:
        c.wait_recv()

    def layer_out(i, _):
        at = pl.ds(pl.multiple_of(i * 128, 128), 128)
        x = state[at, :] + jnp.dot(heads_all[at, :], sout[...], preferred_element_type=F32)
        state[at, :] = x
        power = jnp.mean(x * x, axis=1, keepdims=True)
        normed = (x * lax.rsqrt(power + EPS) * gains_ref[1:2, :]).astype(BF16)
        dkeys[at, :] = jnp.dot(normed, deckv_ref[0], preferred_element_type=F32).astype(BF16)
        vals = jnp.dot(normed, deckv_ref[1], preferred_element_type=F32).astype(BF16).astype(F32)
        vals = vals * readout_ref[...]
        mark = jnp.zeros((128, 128), F32)
        for h in range(nh):
            mark = jnp.where(
                lane == h, jnp.sum(vals[:, h * HEAD : (h + 1) * HEAD], axis=1, keepdims=True), mark
            )
        vread[at, :] = mark
        return 0

    lax.fori_loop(0, lat_rows // 128, layer_out, 0)
    latout_ref[...] = state[:, mycols]
    dkeyst[...] = dkeys[...].astype(F32).T.astype(BF16)

    def decode(i, _):
        at = pl.ds(pl.multiple_of(i * 256, 256), 256)
        mine = jnp.zeros((1, 256), F32)
        for h in range(nh):
            cols = slice(h * HEAD, (h + 1) * HEAD)
            s = lax.dot_general(dkeys[:, cols], query[at, cols], LAST, preferred_element_type=F32) * scale
            e = jnp.exp(s)
            w = e * (1.0 / jnp.sum(e, axis=0, keepdims=True))
            v = vread[:, h : h + 1]
            f = jnp.sum(w * v, axis=0, keepdims=True)
            mine += f
            dqt[cols, at] = jnp.dot(
                dkeyst[cols, :], (w * (v - f)).astype(BF16), preferred_element_type=F32
            )
        fpart[:, at] = jnp.broadcast_to(mine, (8, 256))
        return 0

    lax.fori_loop(0, count // 256, decode, 0)
    fdh = [
        go(put(fpart, fin.at[e], fd_s.at[e], fd_r.at[e], hto[e])) for e in range(1, nhead)
    ]
    for c in fdh:
        c.wait_recv()
    field = fpart[0:1, :]
    for e in range(1, nhead):
        field = field + fin[e, 0:1, :]
    field_ref[...] = field
    dqb[...] = (dqt[...] * ((field - target) * scale)).astype(BF16)

    def gradient(i, _):
        at = pl.ds(pl.multiple_of(i * 512, 512), 512)
        out = jnp.dot(dqb[...], enc[:, at], preferred_element_type=F32)
        gbuf[at, :] = out.T.astype(BF16)
        return 0

    lax.fori_loop(0, features // 512, gradient, 0)

    def partial(q, c, way):
        k = q * 2 + c
        at = pl.ds(q * rows + c * half, half)
        into, sem = (gin, gr_r) if way == 0 else (gin_left, gl_r)
        return put(gbuf.at[at], into.at[q, pl.ds(c * half, half)], gr_s.at[k], sem.at[k], ahead[way])

    def onward(q, c, way):
        at = slice(q * rows + c * half, q * rows + (c + 1) * half)

        @pl.when(has(way, 1))
        def _():
            partial(q, c, way).wait_recv()
            gbuf[at, :] = (
                gbuf[at, :].astype(F32) + (gin, gin_left)[way][q, c * half : (c + 1) * half, :].astype(F32)
            ).astype(BF16)

        partial(q, c, way).start()

    for k in range(npick - 1):
        for c in range(2):
            for way in range(2):
                q = npick - 1 - k if way == 0 else k

                @pl.when(p < q if way == 0 else p > q)
                def _():
                    onward(q, c, way)

    grad_ref[...] = gbuf[pl.ds(mine, rows), :].astype(F32)
    for way in range(2):

        @pl.when(has(way, 1))
        def _():
            for c in range(2):
                k = p * 2 + c
                at = pl.ds(c * half, half)
                ref = (gin if way == 0 else gin_left).at[p, at]
                put(ref, ref, gr_s.at[k], (gr_r if way == 0 else gl_r).at[k], mate).wait_recv()
                grad_ref[at, :] += ref[...].astype(F32)

    for q in range(npick):
        for c in range(2):

            @pl.when(p != q)
            def _():
                partial(q, c, 0).wait_send()

    for c in range(3):
        finish(c)
    for c in sends:
        c.wait_send()


def on_device(
    npick, nhead, coords, horizon_ids, horizon_levels, latents, kv_weight, cross_out, norm_gains,
    self_qkv, self_out, dec_kv, dec_query, readout,
):
    count = coords.shape[1]
    rows, local = dec_query.shape
    lat_rows, width = latents.shape
    features = rows * npick
    share = lat_rows // npick
    wide = -(-2 * npick // 128) * 128
    freq = (0.5 * jnp.linspace(1.0, BANDS / 2.0, BANDS).astype(F32)).reshape(1, BANDS)
    vmem = pl.BlockSpec(memory_space=pltpu.VMEM)
    hbm = pl.BlockSpec(memory_space=pl.ANY)
    dma = lambda n: pltpu.SemaphoreType.DMA((n,))
    scratch = [
        pltpu.VMEM((count, features), BF16),
        pltpu.VMEM((features, 2 * local), BF16),
        pltpu.VMEM((features, local), BF16),
        pltpu.VMEM((width, width), BF16),
        pltpu.VMEM((width, width), BF16),
        pltpu.VMEM((count, 2 * local), BF16),
        pltpu.VMEM((lat_rows, local), BF16),
        pltpu.VMEM((lat_rows, 128), F32),
        pltpu.VMEM((npick, 8, lat_rows), F32),
        pltpu.VMEM((npick, share, local), BF16),
        pltpu.VMEM((wide, lat_rows), F32),
        pltpu.VMEM((lat_rows, wide), F32),
        pltpu.VMEM((lat_rows, width), BF16),
        pltpu.VMEM((lat_rows, width), F32),
        pltpu.VMEM((3, lat_rows, local), BF16),
        pltpu.VMEM((lat_rows, width), BF16),
        pltpu.VMEM((lat_rows, local), BF16),
        pltpu.VMEM((local, lat_rows), BF16),
        pltpu.VMEM((lat_rows, 128), F32),
        pltpu.VMEM((count, local), BF16),
        pltpu.VMEM((local, count), F32),
        pltpu.VMEM((local, count), BF16),
        pltpu.VMEM((8, count), F32),
        pltpu.VMEM((nhead, 8, count), F32),
        pltpu.VMEM((features, local), BF16),
        pltpu.VMEM((npick, rows, local), BF16),
        pltpu.VMEM((npick, rows, local), BF16),
        pltpu.VMEM((local // HEAD, lat_rows, count), BF16),
    ]
    z, h = npick, nhead
    for n in (6 * z, 6 * z, h, h, z, z, z, z * h, h, h, 2 * z):
        scratch += [dma(n), dma(n)]
    scratch += [dma(2 * z), dma(4)]
    field, latents_out, grad = pl.pallas_call(
        functools.partial(kernel, npick, nhead),
        out_shape=(
            jax.ShapeDtypeStruct((1, count), F32),
            jax.ShapeDtypeStruct((lat_rows, local), F32),
            jax.ShapeDtypeStruct((rows, local), F32),
        ),
        in_specs=[vmem] * 5 + [hbm, hbm, vmem, vmem, hbm, vmem, hbm, vmem],
        out_specs=(vmem, vmem, vmem),
        scratch_shapes=scratch,
        compiler_params=pltpu.CompilerParams(
            collective_id=0, has_side_effects=True, vmem_limit_bytes=56 * 2**20
        ),
    )(
        coords.T,
        horizon_ids.reshape(1, count),
        horizon_levels.reshape(-1, 1),
        freq,
        latents,
        kv_weight.reshape(rows, 2 * local),
        cross_out,
        norm_gains,
        self_qkv,
        self_out,
        dec_kv,
        dec_query,
        readout.reshape(1, local),
    )
    return field.reshape(count), latents_out, grad


def solution(mesh):
    in_specs = (
        P(None, ("groups", "picks")),
        P(("groups", "picks")),
        P("groups"),
        P(),
        P("picks", None, "heads"),
        P("heads", None),
        P(),
        P(None, None, "heads"),
        P(None, "heads"),
        P(None, None, "heads"),
        P("picks", "heads"),
        P("heads"),
    )
    out_specs = (P(("groups", "picks")), P("groups", "heads"), P(("groups", "picks"), "heads"))
    return jax.shard_map(
        functools.partial(on_device, mesh.shape["picks"], mesh.shape["heads"]),
        mesh=mesh, in_specs=in_specs, out_specs=out_specs, check_vma=False,
    )
```

```python
import functools

import jax
import jax.numpy as jnp
from jax import lax
from jax.experimental import pallas as pl
from jax.experimental.pallas import tpu as pltpu
from jax.sharding import PartitionSpec as P

HEAD = 128
BANDS = 512
HORIZONS = 64
PI = 3.141592653589793
EPS = 1e-06
F32 = jnp.float32
BF16 = jnp.bfloat16
LAST = (((1,), (1,)), ((), ()))


def sin_half(r):
    u = r * r
    p = 0.07765766 * u - 0.5982913
    p = p * u + 2.55007753
    p = p * u - 5.16771008
    p = p * u + PI
    return p * r


def cos_half(r):
    u = r * r
    p = -0.02439632 * u + 0.23493732
    p = p * u - 1.335212
    p = p * u + 4.05870916
    p = p * u - 4.93480214
    return p * u + 1.0


def kernel(
    npick, nhead,
    coords_ref, ids_ref, levels_ref, freq_ref, latents_ref, kv_in, cross_in, gains_ref,
    qkvw_ref, sout_in, deckv_ref, dq_in, readout_ref,
    field_ref, latout_ref, grad_ref,
    enc, kvw, dqw, cross, sout, kvs, numer, stats, stin, parts, coef, coeft, att, state,
    qkv, heads_all, dkeys, dkeyst, vread, query, dqt, dqb, fpart, fin, gbuf, gin, gin_left, expo,
    wz_s, wz_r, wy_s, wy_r, cr_s, cr_r, so_s, so_r,
    nu_s, nu_r, st_s, st_r, az_s, az_r, ah_s, ah_r, ho_s, ho_r, fd_s, fd_r, gr_s, gr_r, gl_r, loc,
):
    g = lax.axis_index("groups")
    p = lax.axis_index("picks")
    hd = lax.axis_index("heads")
    mate = {"groups": 1 - g}
    scale = HEAD ** (-0.5)
    count, features = enc.shape
    lat_rows, width = latents_ref.shape
    rows = dq_in.shape[0]
    half = rows // 2
    local = dq_in.shape[1]
    nh = local // HEAD
    share = lat_rows // npick
    col = pl.multiple_of(hd * local, HEAD)
    sends = []

    def put(src, dst, ssem, rsem, to):
        return pltpu.make_async_remote_copy(
            src_ref=src, dst_ref=dst, send_sem=ssem, recv_sem=rsem, device_id=to,
            device_id_type=pl.DeviceIdType.MESH,
        )

    def go(copy):
        copy.start()
        sends.append(copy)
        return copy

    zto = [None] + [{"picks": lax.rem(p + d, npick)} for d in range(1, npick)]
    zfrom = [p] + [lax.rem(p + npick - d, npick) for d in range(1, npick)]
    hto = [None] + [{"heads": lax.rem(hd + e, nhead)} for e in range(1, nhead)]

    own = []
    mine = pl.multiple_of(p * rows, 16)
    own.append(pltpu.make_async_copy(kv_in, kvw.at[pl.ds(mine, rows)], loc.at[0]))
    own.append(pltpu.make_async_copy(dq_in, dqw.at[pl.ds(mine, rows)], loc.at[1]))
    own.append(pltpu.make_async_copy(cross_in, cross.at[pl.ds(col, local)], loc.at[2]))
    own.append(pltpu.make_async_copy(sout_in, sout.at[:, pl.ds(col, local)], loc.at[3]))
    for c in own:
        c.start()

    barrier = pltpu.get_barrier_semaphore()
    for to in zto[1:] + hto[1:] + [mate]:
        pl.semaphore_signal(barrier, inc=1, device_id=to, device_id_type=pl.DeviceIdType.MESH)
    pl.semaphore_wait(barrier, npick + nhead - 1)

    spots = [(kv_in, kvw, 0), (kv_in, kvw, local), (dq_in, dqw, 0)]
    ahead = [{"picks": jnp.minimum(p + 1, npick - 1)}, {"picks": jnp.maximum(p - 1, 0)}]
    may = [p + 1 < npick, p > 0]

    def span(owner, part):
        return pl.ds(pl.multiple_of(owner * rows + part * half, 16), half)

    def along(c, way, s):
        _, whole, first = spots[c]
        owner = p - s if way == 0 else p + s
        ref = whole.at[span(owner, g), pl.ds(first, local)]
        k = (c * 2 + way) * npick + s
        return put(ref, ref, wz_s.at[k], wz_r.at[k + 1], ahead[way])

    def start_own(c):
        source, whole, first = spots[c]
        for way in range(2):
            k = (c * 2 + way) * npick

            @pl.when(may[way])
            def _():
                put(
                    source.at[pl.ds(pl.multiple_of(g * half, 16), half), pl.ds(first, local)],
                    whole.at[span(p, g), pl.ds(first, local)],
                    wz_s.at[k], wz_r.at[k + 1], ahead[way],
                ).start()

    def across(c, way, s):
        _, whole, first = spots[c]
        owner = p - s if way == 0 else p + s
        ref = whole.at[span(owner, g), pl.ds(first, local)]
        k = (c * 2 + way) * npick + s
        return put(ref, ref, wy_s.at[k], wy_r.at[k], mate)

    def has(way, s):
        return p - s >= 0 if way == 0 else p + s < npick

    def pass_on(c, s):
        _, whole, first = spots[c]
        for way in range(2):

            @pl.when(has(way, s))
            def _():
                owner = p - s if way == 0 else p + s
                ref = whole.at[span(owner, g), pl.ds(first, local)]
                k = (c * 2 + way) * npick + s
                put(ref, ref, wz_s.at[k], wz_r.at[k], mate).wait_recv()
                across(c, way, s).start()

                if s < npick - 1:

                    @pl.when(may[way])
                    def _():
                        along(c, way, s).start()

    def pass_on_rest(c):
        for s in range(3, npick):
            pass_on(c, s)

    def arrive(c):
        for s in range(1, npick):
            for way in range(2):

                @pl.when(has(way, s))
                def _():
                    across(c, way, s).wait_recv()

    def finish(c):
        for s in range(npick):
            for way in range(2):
                if s < npick - 1:

                    @pl.when(has(way, s) & may[way])
                    def _():
                        along(c, way, s).wait_send()

                if s:

                    @pl.when(has(way, s))
                    def _():
                        across(c, way, s).wait_send()

    start_own(0)
    crh = [
        go(put(cross_in, cross.at[pl.ds(col, local)], cr_s.at[e], cr_r.at[e], hto[e]))
        for e in range(1, nhead)
    ]
    soh = [
        go(put(sout_in, sout.at[:, pl.ds(col, local)], so_s.at[e], so_r.at[e], hto[e]))
        for e in range(1, nhead)
    ]

    tile = 32
    freq = freq_ref[...]

    def encode(i, _):
        at = pl.ds(pl.multiple_of(i * tile, tile), tile)
        for c in range(3):
            turn = coords_ref[at, c : c + 1] * freq
            r = turn - jnp.floor(turn + 0.5)
            s = sin_half(r)
            k = cos_half(r)
            enc[at, c * BANDS : (c + 1) * BANDS] = (2.0 * s * k).astype(BF16)
            enc[at, (3 + c) * BANDS : (4 + c) * BANDS] = (1.0 - 2.0 * s * s).astype(BF16)
        return 0

    steps = count // tile
    lax.fori_loop(0, steps // 3, encode, 0)
    pass_on(0, 1)
    start_own(1)
    lax.fori_loop(steps // 3, 2 * steps // 3, encode, 0)
    if npick > 2:
        pass_on(0, 2)
    lax.fori_loop(2 * steps // 3, steps, encode, 0)
    pass_on_rest(0)
    pass_on(1, 1)
    start_own(2)
    own[0].wait()
    arrive(0)

    def project(first):
        def body(i, _):
            at = pl.ds(pl.multiple_of(i * 256, 256), 256)
            kvs[at, first : first + local] = jnp.dot(
                enc[at, :], kvw[:, first : first + local], preferred_element_type=F32
            ).astype(BF16)
            return 0

        lax.fori_loop(0, count // 256, body, 0)

    project(0)
    if npick > 2:
        pass_on(1, 2)

    lane = lax.broadcasted_iota(jnp.int32, (128, 128), 1)

    def cross_scores(i, _):
        at = pl.ds(pl.multiple_of(i * 128, 128), 128)
        mark = jnp.zeros((128, 128), F32)
        for h in range(nh):
            q = latents_ref[at, pl.ds(pl.multiple_of(col + h * HEAD, HEAD), HEAD)]
            s = lax.dot_general(q, kvs[:, h * HEAD : (h + 1) * HEAD], LAST, preferred_element_type=F32) * scale
            top = jnp.max(s, axis=1, keepdims=True)
            e = jnp.exp(s - top)
            total = jnp.sum(e, axis=1, keepdims=True)
            expo[h, at, :] = e.astype(BF16)
            mark = jnp.where(lane == 2 * h, top, jnp.where(lane == 2 * h + 1, total, mark))
        stats[at, :] = mark
        return 0

    lax.fori_loop(0, lat_rows // 128, cross_scores, 0)
    pass_on_rest(1)
    stin[0] = stats[...].T[:8]
    stz, nuz = [None], [None]
    for d in range(1, npick):
        stz.append(go(put(stin.at[0], stin.at[d], st_s.at[d], st_r.at[d], zto[d])))
    pass_on(2, 1)
    arrive(1)
    project(local)
    if npick > 2:
        pass_on(2, 2)

    def cross_values(i, _):
        at = pl.ds(pl.multiple_of(i * 128, 128), 128)
        for h in range(nh):
            numer[at, h * HEAD : (h + 1) * HEAD] = jnp.dot(
                expo[h, at, :], kvs[:, local + h * HEAD : local + (h + 1) * HEAD], preferred_element_type=F32
            ).astype(BF16)
        return 0

    lax.fori_loop(0, lat_rows // 128, cross_values, 0)
    for d in range(1, npick):
        dst = lax.rem(p + d, npick)
        nuz.append(go(put(
            numer.at[pl.ds(pl.multiple_of(dst * share, 16), share)], parts.at[d],
            nu_s.at[d], nu_r.at[d], zto[d],
        )))
    pass_on_rest(2)
    for d in range(1, npick):
        stz[d].wait_recv()
    coef[...] = jnp.zeros(coef.shape, F32)
    for h in range(nh):
        best = stin[0, 2 * h : 2 * h + 1, :]
        for d in range(1, npick):
            best = jnp.maximum(best, stin[d, 2 * h : 2 * h + 1, :])
        factors = [jnp.exp(stin[d, 2 * h : 2 * h + 1, :] - best) for d in range(npick)]
        total = sum(factors[d] * stin[d, 2 * h + 1 : 2 * h + 2, :] for d in range(npick))
        for d in range(npick):
            coef[2 * d + h : 2 * d + h + 1, :] = factors[d] / total
    coeft[...] = coef[...].T
    myrows = pl.ds(pl.multiple_of(p * share, 16), share)
    factor = coeft[myrows, :]
    for d in range(1, npick):
        nuz[d].wait_recv()
    for h in range(nh):
        cols = slice(h * HEAD, (h + 1) * HEAD)
        acc = numer[myrows, cols].astype(F32) * factor[:, h : h + 1]
        for d in range(1, npick):
            acc += parts[d, :, cols].astype(F32) * factor[:, 2 * d + h : 2 * d + h + 1]
        att[myrows, pl.ds(pl.multiple_of(col + h * HEAD, HEAD), HEAD)] = acc.astype(BF16)
    mycols = pl.ds(col, local)
    azz = [None] + [
        go(put(att.at[myrows, mycols], att.at[myrows, mycols], az_s.at[d], az_r.at[d], zto[d]))
        for d in range(1, npick)
    ]
    ahh = []
    for d in range(npick):
        if d:
            azz[d].wait_recv()
        at = pl.ds(pl.multiple_of(zfrom[d] * share, 16), share)
        for e in range(1, nhead):
            k = d * nhead + e
            ahh.append(go(put(att.at[at, mycols], att.at[at, mycols], ah_s.at[k], ah_r.at[k], hto[e])))
    own[1].wait()
    arrive(2)

    def queries(i, _):
        at = pl.ds(pl.multiple_of(i * 256, 256), 256)
        query[at, :] = jnp.dot(enc[at, :], dqw[...], preferred_element_type=F32).astype(BF16)
        return 0

    lax.fori_loop(0, count // 256, queries, 0)
    own[2].wait()
    for c in crh + ahh:
        c.wait_recv()

    def layer_in(i, _):
        at = pl.ds(pl.multiple_of(i * 128, 128), 128)
        x = latents_ref[at, :].astype(F32) + jnp.dot(att[at, :], cross[...], preferred_element_type=F32)
        state[at, :] = x
        power = jnp.mean(x * x, axis=1, keepdims=True)
        normed = (x * lax.rsqrt(power + EPS) * gains_ref[0:1, :]).astype(BF16)
        for j in range(3):
            qkv[j, at, :] = jnp.dot(normed, qkvw_ref[j], preferred_element_type=F32).astype(BF16)
        return 0

    lax.fori_loop(0, lat_rows // 128, layer_in, 0)

    def self_attention(i, _):
        at = pl.ds(pl.multiple_of(i * 128, 128), 128)
        for h in range(nh):
            cols = slice(h * HEAD, (h + 1) * HEAD)
            s = lax.dot_general(qkv[0, at, cols], qkv[1, :, cols], LAST, preferred_element_type=F32) * scale
            e = jnp.exp(s)
            probs = (e * (1.0 / jnp.sum(e, axis=1, keepdims=True))).astype(BF16)
            heads_all[at, pl.ds(pl.multiple_of(col + h * HEAD, HEAD), HEAD)] = jnp.dot(
                probs, qkv[2, :, cols], preferred_element_type=F32
            ).astype(BF16)
        return 0

    lax.fori_loop(0, lat_rows // 128, self_attention, 0)
    hoh = [
        go(put(heads_all.at[:, mycols], heads_all.at[:, mycols], ho_s.at[e], ho_r.at[e], hto[e]))
        for e in range(1, nhead)
    ]
    horizon = lax.broadcasted_iota(jnp.int32, (HORIZONS, count), 0)
    target = jnp.sum(jnp.where(horizon == ids_ref[...], levels_ref[...], 0.0), axis=0, keepdims=True)
    own[3].wait()
    for c in soh + hoh:
        c.wait_recv()

    def layer_out(i, _):
        at = pl.ds(pl.multiple_of(i * 128, 128), 128)
        x = state[at, :] + jnp.dot(heads_all[at, :], sout[...], preferred_element_type=F32)
        state[at, :] = x
        power = jnp.mean(x * x, axis=1, keepdims=True)
        normed = (x * lax.rsqrt(power + EPS) * gains_ref[1:2, :]).astype(BF16)
        dkeys[at, :] = jnp.dot(normed, deckv_ref[0], preferred_element_type=F32).astype(BF16)
        vals = jnp.dot(normed, deckv_ref[1], preferred_element_type=F32).astype(BF16).astype(F32)
        vals = vals * readout_ref[...]
        mark = jnp.zeros((128, 128), F32)
        for h in range(nh):
            mark = jnp.where(
                lane == h, jnp.sum(vals[:, h * HEAD : (h + 1) * HEAD], axis=1, keepdims=True), mark
            )
        vread[at, :] = mark
        return 0

    lax.fori_loop(0, lat_rows // 128, layer_out, 0)
    latout_ref[...] = state[:, mycols]
    dkeyst[...] = dkeys[...].astype(F32).T.astype(BF16)

    def decode(i, _):
        at = pl.ds(pl.multiple_of(i * 256, 256), 256)
        mine = jnp.zeros((1, 256), F32)
        for h in range(nh):
            cols = slice(h * HEAD, (h + 1) * HEAD)
            s = lax.dot_general(dkeys[:, cols], query[at, cols], LAST, preferred_element_type=F32) * scale
            e = jnp.exp(s)
            w = e * (1.0 / jnp.sum(e, axis=0, keepdims=True))
            v = vread[:, h : h + 1]
            f = jnp.sum(w * v, axis=0, keepdims=True)
            mine += f
            dqt[cols, at] = jnp.dot(
                dkeyst[cols, :], (w * (v - f)).astype(BF16), preferred_element_type=F32
            )
        fpart[:, at] = jnp.broadcast_to(mine, (8, 256))
        return 0

    lax.fori_loop(0, count // 256, decode, 0)
    fdh = [
        go(put(fpart, fin.at[e], fd_s.at[e], fd_r.at[e], hto[e])) for e in range(1, nhead)
    ]
    for c in fdh:
        c.wait_recv()
    field = fpart[0:1, :]
    for e in range(1, nhead):
        field = field + fin[e, 0:1, :]
    field_ref[...] = field
    dqb[...] = (dqt[...] * ((field - target) * scale)).astype(BF16)

    def gradient(i, _):
        at = pl.ds(pl.multiple_of(i * 512, 512), 512)
        out = jnp.dot(dqb[...], enc[:, at], preferred_element_type=F32)
        gbuf[at, :] = out.T.astype(BF16)
        return 0

    by_block = rows % 256 == 0
    if not by_block:
        lax.fori_loop(0, features // 512, gradient, 0)

    def gradient_block(q):
        def body(i, _):
            at = pl.ds(pl.multiple_of(q * rows + i * 256, 256), 256)
            out = jnp.dot(dqb[...], enc[:, at], preferred_element_type=F32)
            gbuf[at, :] = out.T.astype(BF16)
            return 0

        if by_block:
            lax.fori_loop(0, rows // 256, body, 0)

    def partial(q, c, way):
        k = q * 2 + c
        at = pl.ds(q * rows + c * half, half)
        into, sem = (gin, gr_r) if way == 0 else (gin_left, gl_r)
        return put(gbuf.at[at], into.at[q, pl.ds(c * half, half)], gr_s.at[k], sem.at[k], ahead[way])

    def onward(q, c, way):
        at = slice(q * rows + c * half, q * rows + (c + 1) * half)

        @pl.when(has(way, 1))
        def _():
            partial(q, c, way).wait_recv()
            gbuf[at, :] = (
                gbuf[at, :].astype(F32) + (gin, gin_left)[way][q, c * half : (c + 1) * half, :].astype(F32)
            ).astype(BF16)

        partial(q, c, way).start()

    for k in range(npick - 1):
        for c in range(2):
            for way in range(2):
                q = npick - 1 - k if way == 0 else k

                @pl.when(p < q if way == 0 else p > q)
                def _():
                    if c == 0:
                        gradient_block(q)
                    onward(q, c, way)

    gradient_block(p)
    grad_ref[...] = gbuf[pl.ds(mine, rows), :].astype(F32)
    for way in range(2):

        @pl.when(has(way, 1))
        def _():
            for c in range(2):
                k = p * 2 + c
                at = pl.ds(c * half, half)
                ref = (gin if way == 0 else gin_left).at[p, at]
                put(ref, ref, gr_s.at[k], (gr_r if way == 0 else gl_r).at[k], mate).wait_recv()
                grad_ref[at, :] += ref[...].astype(F32)

    for q in range(npick):
        for c in range(2):

            @pl.when(p != q)
            def _():
                partial(q, c, 0).wait_send()

    for c in range(3):
        finish(c)
    for c in sends:
        c.wait_send()


def on_device(
    npick, nhead, coords, horizon_ids, horizon_levels, latents, kv_weight, cross_out, norm_gains,
    self_qkv, self_out, dec_kv, dec_query, readout,
):
    count = coords.shape[1]
    rows, local = dec_query.shape
    lat_rows, width = latents.shape
    features = rows * npick
    share = lat_rows // npick
    wide = -(-2 * npick // 128) * 128
    freq = (0.5 * jnp.linspace(1.0, BANDS / 2.0, BANDS).astype(F32)).reshape(1, BANDS)
    vmem = pl.BlockSpec(memory_space=pltpu.VMEM)
    hbm = pl.BlockSpec(memory_space=pl.ANY)
    dma = lambda n: pltpu.SemaphoreType.DMA((n,))
    scratch = [
        pltpu.VMEM((count, features), BF16),
        pltpu.VMEM((features, 2 * local), BF16),
        pltpu.VMEM((features, local), BF16),
        pltpu.VMEM((width, width), BF16),
        pltpu.VMEM((width, width), BF16),
        pltpu.VMEM((count, 2 * local), BF16),
        pltpu.VMEM((lat_rows, local), BF16),
        pltpu.VMEM((lat_rows, 128), F32),
        pltpu.VMEM((npick, 8, lat_rows), F32),
        pltpu.VMEM((npick, share, local), BF16),
        pltpu.VMEM((wide, lat_rows), F32),
        pltpu.VMEM((lat_rows, wide), F32),
        pltpu.VMEM((lat_rows, width), BF16),
        pltpu.VMEM((lat_rows, width), F32),
        pltpu.VMEM((3, lat_rows, local), BF16),
        pltpu.VMEM((lat_rows, width), BF16),
        pltpu.VMEM((lat_rows, local), BF16),
        pltpu.VMEM((local, lat_rows), BF16),
        pltpu.VMEM((lat_rows, 128), F32),
        pltpu.VMEM((count, local), BF16),
        pltpu.VMEM((local, count), F32),
        pltpu.VMEM((local, count), BF16),
        pltpu.VMEM((8, count), F32),
        pltpu.VMEM((nhead, 8, count), F32),
        pltpu.VMEM((features, local), BF16),
        pltpu.VMEM((npick, rows, local), BF16),
        pltpu.VMEM((npick, rows, local), BF16),
        pltpu.VMEM((local // HEAD, lat_rows, count), BF16),
    ]
    z, h = npick, nhead
    for n in (6 * z, 6 * z, h, h, z, z, z, z * h, h, h, 2 * z):
        scratch += [dma(n), dma(n)]
    scratch += [dma(2 * z), dma(4)]
    field, latents_out, grad = pl.pallas_call(
        functools.partial(kernel, npick, nhead),
        out_shape=(
            jax.ShapeDtypeStruct((1, count), F32),
            jax.ShapeDtypeStruct((lat_rows, local), F32),
            jax.ShapeDtypeStruct((rows, local), F32),
        ),
        in_specs=[vmem] * 5 + [hbm, hbm, vmem, vmem, hbm, vmem, hbm, vmem],
        out_specs=(vmem, vmem, vmem),
        scratch_shapes=scratch,
        compiler_params=pltpu.CompilerParams(
            collective_id=0, has_side_effects=True, vmem_limit_bytes=56 * 2**20
        ),
    )(
        coords.T,
        horizon_ids.reshape(1, count),
        horizon_levels.reshape(-1, 1),
        freq,
        latents,
        kv_weight.reshape(rows, 2 * local),
        cross_out,
        norm_gains,
        self_qkv,
        self_out,
        dec_kv,
        dec_query,
        readout.reshape(1, local),
    )
    return field.reshape(count), latents_out, grad


def solution(mesh):
    in_specs = (
        P(None, ("groups", "picks")),
        P(("groups", "picks")),
        P("groups"),
        P(),
        P("picks", None, "heads"),
        P("heads", None),
        P(),
        P(None, None, "heads"),
        P(None, "heads"),
        P(None, None, "heads"),
        P("picks", "heads"),
        P("heads"),
    )
    out_specs = (P(("groups", "picks")), P("groups", "heads"), P(("groups", "picks"), "heads"))
    return jax.shard_map(
        functools.partial(on_device, mesh.shape["picks"], mesh.shape["heads"]),
        mesh=mesh, in_specs=in_specs, out_specs=out_specs, check_vma=False,
    )
```
